256 devices in a mesh: docs: 128 (over x, y, z), rep: 2 (over core).
Axes of the slice: x: 4, y: 4, z: 8, core: 2. Of those that a mesh axis runs over, the one named last changes fastest.
Arguments:
- slab: bfloat16 [131072, 768], P(('docs', 'rep')), may hold values from -9 to 9
- old_cluster: int32 [131072, 1], P(('docs', 'rep')), may hold values from 0 to 127; in each aligned block of 512 rows (0 to 511, 512 to 1023, ...) at most 8 rows name the same one
- new_cluster: int32 [131072, 1], P(('docs', 'rep')), may hold values from 0 to 127; in each aligned block of 512 rows (0 to 511, 512 to 1023, ...) at most 8 rows name the same one
- anchor_ids: int32 [128, 1536], P('docs', 'rep'), may hold values from 0 to 511
- anchor_new: bfloat16 [128, 1536, 768], P('docs', 'rep'), may hold values from -9 to 9
- owner_table: int32 [128], replicated, may hold values from 0 to 127, each once
Outputs:
- relayed: bfloat16 [128, 2048, 768], P('docs', 'rep')
The draws below stay inside these ranges and needn't reach their ends.
Inputs may be any that keep to these rules, and one draw needn't show every extreme that they name: `anchor_ids`: column c of a cluster's list names a row of block (s * 2 + r) as in the reference program, by its number within the block. `old_cluster`: the 512 documents of one device name each cluster at most 8 times. `new_cluster`: the 512 documents of one device name each new cluster at most 8 times. `owner_table`: every docs index owns exactly one new cluster.
All inputs are finite; a program needn't handle non-finite values.
Results may differ from the reference program's by a relative error of at most 0.022.
Values may be sent and summed in bfloat16 or wider, within the bound.
No kernel may reach another device: no remote copies, remote signals or barrier semaphores. Data moves between devices by JAX's collectives and lax.ppermute only.
A program may use at most 64 MiB of HBM per device.

```python
import math
import jax
import jax.numpy as jnp
import numpy as np
from jax import lax

D = 768
ITERS = 3
A = 1536
ROWS_DEV = 512
CLUSTERS = 128
CAP = 8
APD = 6
ROWS = 131072
N_DOCS = 128
N_REP = 2


def draw_slab(key, part):
    key = jax.random.fold_in(key, 11)
    values = jnp.clip(jax.random.normal(key, (ROWS, D), jnp.float32), -6.0, 6.0)
    return values.astype(jnp.bfloat16)


def draw_anchor_new(key, part):
    key = jax.random.fold_in(key, 23)
    values = jnp.clip(jax.random.normal(key, (CLUSTERS, A, D), jnp.float32), -6.0, 6.0)
    return values.astype(jnp.bfloat16)


def plant(array, key, low, largest):
    longest = array.shape.index(max(array.shape))
    spots = []
    for shift in (0, 1):
        where = [jax.random.randint(jax.random.fold_in(key, axis), (), 0, length) for axis, length in enumerate(array.shape)]
        where[longest] = (where[longest] + shift) % array.shape[longest]
        spots.append(tuple(where))
    return array.at[spots[0]].set(low).at[spots[1]].set(largest)


def deal_out(key, own, number, rows, amount, top, most, slope):
    order = jax.random.permutation(key, amount)
    packed, ordinary = portions_of(amount, rows * top, most, slope, True), portions_of(amount, rows * top, most, slope, False)
    places = jnp.arange(amount)

    def named(tallies, offset_by):
        used = int((tallies > 0).sum())
        fixed = max(1, used // 4)
        moved = fixed + (places - fixed + offset_by * (used - fixed)) % max(1, amount - fixed)
        return jnp.zeros((amount,), jnp.int32).at[order[jnp.where(places < fixed, places, moved)]].set(jnp.asarray(tallies, jnp.int32))

    tallies = jnp.where(number % 4 == 0, named(packed, number // 4), named(ordinary, number - number // 4 - 1))
    mixed = jax.random.permutation(jax.random.fold_in(own, 3), amount)
    source_of, sink = mixed[0:amount // 2 * 2:2], mixed[1:amount // 2 * 2:2]
    room = jnp.minimum(tallies[source_of] - 1, most - tallies[sink]) // 2
    room = jnp.where((source_of == order[0]) | (sink == order[0]) | (tallies[sink] == 0), 0, jnp.maximum(room, 0))
    moved = jax.random.randint(jax.random.fold_in(own, 4), (amount // 2,), 0, 1 << 20) % (room + 1)
    tallies = tallies.at[source_of].add(-moved).at[sink].add(moved)
    items = jnp.searchsorted(jnp.cumsum(tallies), jnp.arange(rows * top), side="right").astype(jnp.int32)
    listing = items.reshape(top, rows).T
    listing = listing[jax.random.permutation(jax.random.fold_in(own, 1), rows)]
    offset_by = jax.random.randint(jax.random.fold_in(own, 2), (rows, 1), 0, top)
    return jnp.take_along_axis(listing, (jnp.arange(top)[None, :] + offset_by) % top, axis=1)


def portions_of(count, total, bound, lean, full):
    portions = [(1 << 20) // math.isqrt(standing ** lean) + 1 for standing in range(1, count + 1)]
    largest = bound if full else min(bound, max(-(-total // count), total * portions[0] // sum(portions)))
    least = 1 if total - largest >= count - 1 else 0
    holding, rest = [largest] + [least] * (count - 1), total - largest - least * (count - 1)
    while rest > 0:
        free = [i for i in range(1, count) if holding[i] < largest] or [i for i in range(1, count) if holding[i] < bound]
        mass, remaining = sum([portions[i] for i in free]), rest
        for i in free:
            addition = min(bound - holding[i], max(1, remaining * portions[i] // mass), rest)
            holding[i] = holding[i] + addition
            rest = rest - addition
    return np.array(holding)


def setup_inputs(seed: int = 0) -> dict:
    splits = jax.random.split(jax.random.key(seed), 7)
    slab = draw_slab(jax.random.fold_in(splits[6], 71), 0)
    old_cluster_keys = jax.random.split(jax.random.fold_in(splits[1], 1), ROWS // ROWS_DEV)
    old_cluster_turns = jax.random.permutation(jax.random.fold_in(splits[1], 3), ROWS // ROWS_DEV)
    old_cluster = jax.vmap(lambda own, number: deal_out(jax.random.fold_in(splits[1], 2), own, number, ROWS_DEV, CLUSTERS, 1, CAP, 2))(old_cluster_keys, old_cluster_turns).reshape((ROWS, 1))
    new_cluster_keys = jax.random.split(jax.random.fold_in(splits[2], 1), ROWS // ROWS_DEV)
    new_cluster_turns = jax.random.permutation(jax.random.fold_in(splits[2], 3), ROWS // ROWS_DEV)
    new_cluster = jax.vmap(lambda own, number: deal_out(jax.random.fold_in(splits[2], 2), own, number, ROWS_DEV, CLUSTERS, 1, CAP, 1))(new_cluster_keys, new_cluster_turns).reshape((ROWS, 1))
    anchor_ids = plant(jax.random.randint(splits[3], (CLUSTERS, A), 0, ROWS_DEV), jax.random.fold_in(splits[3], 1), 0, ROWS_DEV - 1).astype(jnp.int32)
    anchor_new = draw_anchor_new(jax.random.fold_in(splits[6], 71), 0)
    owner_table = jax.random.permutation(splits[5], CLUSTERS).astype(jnp.int32)
    return dict(slab=slab, old_cluster=old_cluster, new_cluster=new_cluster, anchor_ids=anchor_ids, anchor_new=anchor_new, owner_table=owner_table)


EPS = 1e-06
polar_scale = 0.3

def polar_fit(gram):
    factor = polar_scale * math.sqrt(D) * lax.rsqrt(jnp.sum(gram * gram) + EPS)
    iterate = (gram * factor).astype(jnp.bfloat16)
    for step in range(ITERS):
        square = jnp.dot(iterate, iterate.T, preferred_element_type=jnp.float32).astype(jnp.bfloat16)
        update = jnp.dot(square, iterate, preferred_element_type=jnp.float32)
        iterate = (1.5 * iterate.astype(jnp.float32) - 0.5 * update).astype(jnp.bfloat16)
    return iterate

def slot_ranks(labels):
    onehot = (labels[:, None] == jnp.arange(N_DOCS, dtype=jnp.int32)[None, :]).astype(jnp.int32)
    earlier = jnp.cumsum(onehot, axis=0) - onehot
    return lax.optimization_barrier(jnp.sum(earlier * onehot, axis=1)).astype(jnp.int32)

def reference(slab, old_cluster, new_cluster, anchor_ids, anchor_new, owner_table):
    blocks = N_DOCS * N_REP
    half = A // N_REP
    column = jnp.arange(A, dtype=jnp.int32)
    rep_of = column // half
    src_of = column % half // APD
    base = (src_of * N_REP + rep_of) * ROWS_DEV
    global_ids = (anchor_ids + base[None, :]).astype(jnp.int32)

    def fit_cluster(k):
        rows = jnp.take(slab, global_ids[k], axis=0)
        gram = jnp.einsum('ad,ae->de', rows.astype(jnp.float32), anchor_new[k].astype(jnp.float32))
        return polar_fit(gram)
    rotations = lax.map(fit_cluster, jnp.arange(N_DOCS, dtype=jnp.int32))
    old_labels = old_cluster[:, 0].reshape(blocks, ROWS_DEV)
    old_ranks = lax.map(slot_ranks, old_labels)
    block_ids = jnp.arange(blocks, dtype=jnp.int32)
    local_ids = jnp.arange(ROWS_DEV, dtype=jnp.int32)
    slot_row = jnp.full((blocks, N_DOCS * CAP), ROWS, jnp.int32)
    slot_row = slot_row.at[block_ids[:, None], old_labels * CAP + old_ranks].set(block_ids[:, None] * ROWS_DEV + local_ids[None, :])
    by_cluster = slot_row.reshape(blocks, N_DOCS, CAP).transpose(1, 0, 2).reshape(N_DOCS, blocks * CAP)

    def map_cluster(mapped, k):
        ids = by_cluster[k]
        rows = jnp.take(slab, ids, axis=0, mode='clip')
        moved = jnp.dot(rows, rotations[k], preferred_element_type=jnp.float32).astype(jnp.bfloat16)
        return (mapped.at[ids].set(moved, mode='drop'), None)
    mapped, unused = lax.scan(map_cluster, jnp.zeros((ROWS, D), jnp.bfloat16), jnp.arange(N_DOCS, dtype=jnp.int32))
    new_labels = new_cluster[:, 0].reshape(blocks, ROWS_DEV)
    new_ranks = lax.map(slot_ranks, new_labels)
    owners = owner_table[new_labels]
    rep_idx = block_ids % N_REP
    src_idx = block_ids // N_REP
    target = rep_idx[:, None] * (N_DOCS * CAP) + src_idx[:, None] * CAP + new_ranks
    relayed = jnp.zeros((N_DOCS, N_REP * N_DOCS * CAP, D), jnp.bfloat16)
    relayed = relayed.at[owners, target].set(mapped.reshape(blocks, ROWS_DEV, D))
    return relayed
```

```python
import math

import jax
import jax.numpy as jnp
from jax import lax
from jax.sharding import PartitionSpec as P

ITERS = 3


EPS = 1e-06
polar_scale = 0.3

bf16 = jnp.bfloat16
f32 = jnp.float32


def one_hot(targets, count):
    return jnp.arange(count, dtype=jnp.int32)[:, None] == targets[None, :]


def slot_ranks(labels, count):
    rows = labels.shape[0]
    onehot = (labels[:, None] == jnp.arange(count, dtype=jnp.int32)[None, :]).astype(bf16)
    order = jnp.arange(rows, dtype=jnp.int32)
    before = (order[None, :] < order[:, None]).astype(bf16)
    earlier = jnp.dot(before, onehot, preferred_element_type=f32)
    return jnp.sum(earlier * onehot.astype(f32), axis=1).astype(jnp.int32)


def select_rows(marks, rows):
    return jnp.dot(marks.astype(bf16), rows, preferred_element_type=f32).astype(bf16)


def newton_step(x):
    square = jnp.einsum("id,jd->ij", x, x, preferred_element_type=f32).astype(bf16)
    update = jnp.dot(square, x, preferred_element_type=f32)
    return (1.5 * x.astype(f32) - 0.5 * update).astype(bf16)


def shards(slab, old_cluster, new_cluster, anchor_ids, anchor_new, owner_table):
    docs_count = lax.axis_size("docs")
    row_count, width = slab.shape
    capacity = 2 * row_count // docs_count
    slots = docs_count * capacity
    half = anchor_ids.shape[1]
    per_source = half // docs_count
    asked = lax.all_to_all(
        anchor_ids.reshape(docs_count, per_source), "docs", split_axis=0, concat_axis=0, tiled=True
    ).reshape(-1)
    picked = select_rows(asked[:, None] == jnp.arange(row_count, dtype=jnp.int32)[None, :], slab)
    fetched = lax.all_to_all(
        picked.reshape(docs_count, per_source // 2, 2, width), "docs", split_axis=0, concat_axis=0, tiled=True
    )
    partial_gram = jnp.einsum(
        "ad,ae->de", fetched.reshape(half, width), anchor_new[0], preferred_element_type=f32
    )
    gram = partial_gram + lax.ppermute(partial_gram, "rep", [(0, 1), (1, 0)])
    factor = polar_scale * math.sqrt(width) * lax.rsqrt(jnp.sum(gram * gram) + EPS)
    iterate = (gram * factor).astype(bf16)
    for step in range(ITERS):
        iterate = newton_step(iterate)

    old_labels = old_cluster[:, 0]
    old_slot = old_labels * capacity + slot_ranks(old_labels, docs_count)
    outgoing = select_rows(one_hot(old_slot, slots), slab).reshape(docs_count, capacity, width)
    arrived = lax.all_to_all(outgoing, "docs", split_axis=0, concat_axis=0, tiled=True)

    new_labels = new_cluster[:, 0]
    matches = new_labels[:, None] == jnp.arange(owner_table.shape[0], dtype=jnp.int32)[None, :]
    owners = jnp.sum(jnp.where(matches, owner_table[None, :], 0), axis=1)
    new_slot = owners * capacity + slot_ranks(new_labels, docs_count)
    source = jnp.sum(jnp.where(one_hot(new_slot, slots), old_slot[None, :] + 1, 0), axis=1) - 1

    flat = arrived.reshape(-1, width)
    moved = jnp.dot(flat, iterate, preferred_element_type=f32).astype(bf16)
    returned = lax.all_to_all(
        moved.reshape(arrived.shape), "docs", split_axis=0, concat_axis=0, tiled=True
    ).reshape(-1, width)
    onward = select_rows(source[:, None] == jnp.arange(slots, dtype=jnp.int32)[None, :], returned)
    onward = onward.reshape(docs_count, capacity, width)
    arrived_rows = lax.all_to_all(onward, "docs", split_axis=0, concat_axis=0, tiled=True)
    return arrived_rows.reshape(1, slots, width)


def solution(mesh):
    in_specs = (
        P(("docs", "rep"), None),
        P(("docs", "rep"), None),
        P(("docs", "rep"), None),
        P("docs", "rep"),
        P("docs", "rep", None),
        P(),
    )
    out_specs = P("docs", "rep", None)
    return jax.shard_map(shards, mesh=mesh, in_specs=in_specs, out_specs=out_specs, check_vma=False)
```

```python
import math

import jax
import jax.numpy as jnp
from jax import lax
from jax.experimental import pallas as pl
from jax.experimental.pallas import tpu as pltpu
from jax.sharding import Mesh, PartitionSpec as P

ITERS = 3
DEPTH = 8
DOCS = ("x", "y", "z")


EPS = 1e-06
polar_scale = 0.3

bf16 = jnp.bfloat16
f32 = jnp.float32


def one_hot(targets, count):
    return jnp.arange(count, dtype=jnp.int32)[:, None] == targets[None, :]


def slot_ranks(labels, count):
    rows = labels.shape[0]
    onehot = (labels[:, None] == jnp.arange(count, dtype=jnp.int32)[None, :]).astype(bf16)
    order = jnp.arange(rows, dtype=jnp.int32)
    before = (order[None, :] < order[:, None]).astype(bf16)
    earlier = jnp.dot(before, onehot, preferred_element_type=f32)
    return jnp.sum(earlier * onehot.astype(f32), axis=1).astype(jnp.int32)


def select_rows(marks, rows):
    return jnp.dot(marks.astype(bf16), rows, preferred_element_type=f32).astype(bf16)


def fit_kernel(own_gram, rows, targets, rotation, gram, iterate, square):
    width = own_gram.shape[0]
    gram[...] = own_gram[...] + lax.dot_general(
        rows[...], targets[...], (((0,), (0,)), ((), ())), preferred_element_type=f32
    )
    total = jnp.sum(gram[...] * gram[...])
    factor = polar_scale * math.sqrt(width) * lax.rsqrt(total + EPS)
    iterate[...] = (gram[...] * factor).astype(bf16)
    for step in range(ITERS):
        square[...] = lax.dot_general(
            iterate[...], iterate[...], (((1,), (1,)), ((), ())), preferred_element_type=f32
        ).astype(bf16)
        update = jnp.dot(square[...], iterate[...], preferred_element_type=f32)
        later = (1.5 * iterate[...].astype(f32) - 0.5 * update).astype(bf16)
        if step < ITERS - 1:
            iterate[...] = later
        else:
            rotation[...] = later


def fit(own_gram, rows, targets):
    width = own_gram.shape[0]
    whole = pl.BlockSpec(memory_space=pltpu.VMEM)
    return pl.pallas_call(
        fit_kernel,
        out_shape=jax.ShapeDtypeStruct((width, width), bf16),
        in_specs=[whole] * 3,
        out_specs=whole,
        scratch_shapes=[
            pltpu.VMEM((width, width), f32),
            pltpu.VMEM((width, width), bf16),
            pltpu.VMEM((width, width), bf16),
        ],
        compiler_params=pltpu.CompilerParams(vmem_limit_bytes=32 * 2**20),
        cost_estimate=pl.CostEstimate(
            flops=2 * (rows.shape[0] * width**2 + 2 * ITERS * width**3), bytes_accessed=6 * 2**20, transcendentals=1
        ),
    )(own_gram, rows, targets)


def map_kernel(arrived, rotation, moved):
    moved[...] = jnp.dot(arrived[...], rotation[...], preferred_element_type=f32).astype(bf16)


def map_rows(arrived, rotation):
    rows, width = arrived.shape
    tile = rows // 4
    return pl.pallas_call(
        map_kernel,
        grid=(rows // tile,),
        out_shape=jax.ShapeDtypeStruct((rows, width), bf16),
        in_specs=[pl.BlockSpec((tile, width), lambda i: (i, 0)), pl.BlockSpec(memory_space=pltpu.VMEM)],
        out_specs=pl.BlockSpec((tile, width), lambda i: (i, 0)),
        compiler_params=pltpu.CompilerParams(vmem_limit_bytes=16 * 2**20),
        cost_estimate=pl.CostEstimate(flops=2 * rows * width**2, bytes_accessed=5 * 2**20, transcendentals=0),
    )(arrived, rotation)


def shards(slab, old_cluster, new_cluster, anchor_ids, anchor_new, owner_table):
    docs_count = lax.axis_size(DOCS)
    row_count, width = slab.shape
    capacity = 2 * row_count // docs_count
    slots = docs_count * capacity
    half = anchor_ids.shape[1]
    per_source = half // docs_count

    def exchange(x):
        return lax.all_to_all(x, DOCS, split_axis=0, concat_axis=0, tiled=True)

    def swap(x):
        return lax.ppermute(x, "rep", [(0, 1), (1, 0)])

    asked = exchange(anchor_ids.reshape(docs_count, per_source)).reshape(-1)
    picked = select_rows(asked[:, None] == jnp.arange(row_count, dtype=jnp.int32)[None, :], slab)
    fetched = exchange(picked.reshape(docs_count, per_source // 2, 2, width))
    other_new = swap(anchor_new[0])

    old_labels = old_cluster[:, 0]
    old_slot = old_labels * capacity + slot_ranks(old_labels, docs_count)
    outgoing = select_rows(one_hot(old_slot, slots), slab).reshape(docs_count, capacity, width)
    fetched, outgoing, other_new = lax.optimization_barrier((fetched, outgoing, other_new))
    arrived = exchange(outgoing).reshape(slots, width)

    fetched = fetched.reshape(half, width)
    other = swap(fetched)
    own_gram = jnp.einsum("ad,ae->de", fetched, anchor_new[0], preferred_element_type=f32)
    rotation = fit(own_gram, other, other_new)
    moved = map_rows(arrived, rotation)

    new_labels = new_cluster[:, 0]
    matches = new_labels[:, None] == jnp.arange(owner_table.shape[0], dtype=jnp.int32)[None, :]
    owners = jnp.sum(jnp.where(matches, owner_table[None, :], 0), axis=1)
    new_slot = owners * capacity + slot_ranks(new_labels, docs_count)
    source = jnp.sum(jnp.where(one_hot(new_slot, slots), old_slot[None, :] + 1, 0), axis=1) - 1

    returned = exchange(moved.reshape(docs_count, capacity, width)).reshape(slots, width)
    onward = select_rows(source[:, None] == jnp.arange(slots, dtype=jnp.int32)[None, :], returned)
    arrived_rows = exchange(onward.reshape(docs_count, capacity, width))
    return arrived_rows.reshape(1, slots, width)


def solution(mesh):
    docs_count, reps = mesh.devices.shape
    side = math.isqrt(docs_count // DEPTH)
    mesh = Mesh(mesh.devices.reshape(side, side, DEPTH, reps), DOCS + ("rep",))
    in_specs = (
        P(DOCS + ("rep",), None),
        P(DOCS + ("rep",), None),
        P(DOCS + ("rep",), None),
        P(DOCS, "rep"),
        P(DOCS, "rep", None),
        P(),
    )
    out_specs = P(DOCS, "rep", None)
    return jax.shard_map(shards, mesh=mesh, in_specs=in_specs, out_specs=out_specs, check_vma=False)
```

```python
import math

import jax
import jax.numpy as jnp
from jax import lax
from jax.experimental import pallas as pl
from jax.experimental.pallas import tpu as pltpu
from jax.sharding import Mesh, PartitionSpec as P

ITERS = 3
DEPTH = 8
DOCS = ("x", "y", "z")
TILES = 4
HEAD_START = 3
MAP_PASSES = 4


EPS = 1e-06
polar_scale = 0.3

bf16 = jnp.bfloat16
f32 = jnp.float32


def select_rows(marks, rows):
    return jnp.dot(marks.astype(bf16), rows, preferred_element_type=f32).astype(bf16)


def fit_kernel(own_gram, rows, targets, rotation, gram, iterate, square):
    width = own_gram.shape[0]
    gram[...] = own_gram[...] + lax.dot_general(
        rows[...], targets[...], (((0,), (0,)), ((), ())), preferred_element_type=f32
    )
    total = jnp.sum(gram[...] * gram[...])
    factor = polar_scale * math.sqrt(width) * lax.rsqrt(total + EPS)
    iterate[...] = (gram[...] * factor).astype(bf16)
    for step in range(ITERS):
        square[...] = lax.dot_general(
            iterate[...], iterate[...], (((1,), (1,)), ((), ())), preferred_element_type=f32
        ).astype(bf16)
        update = jnp.dot(square[...], iterate[...], preferred_element_type=f32)
        later = (1.5 * iterate[...].astype(f32) - 0.5 * update).astype(bf16)
        if step < ITERS - 1:
            iterate[...] = later
        else:
            rotation[...] = later


def fit(own_gram, rows, targets):
    width = own_gram.shape[0]
    whole = pl.BlockSpec(memory_space=pltpu.VMEM)
    return pl.pallas_call(
        fit_kernel,
        out_shape=jax.ShapeDtypeStruct((width, width), bf16),
        in_specs=[whole] * 3,
        out_specs=whole,
        scratch_shapes=[
            pltpu.VMEM((width, width), f32),
            pltpu.VMEM((width, width), bf16),
            pltpu.VMEM((width, width), bf16),
        ],
        compiler_params=pltpu.CompilerParams(vmem_limit_bytes=32 * 2**20),
        cost_estimate=pl.CostEstimate(
            flops=2 * (rows.shape[0] * width**2 + 2 * ITERS * width**3), bytes_accessed=6 * 2**20, transcendentals=1
        ),
    )(own_gram, rows, targets)


def map_kernel(passes, arrived, rotation, moved):
    @pl.loop(0, passes[0])
    def _(_):
        moved[...] = jnp.dot(arrived[...], rotation[...], preferred_element_type=f32).astype(bf16)


def map_rows(passes, arrived, rotation):
    rows, width = arrived.shape
    tile = rows // TILES
    return pl.pallas_call(
        map_kernel,
        grid=(TILES,),
        out_shape=pltpu.HBM((rows, width), bf16),
        in_specs=[
            pl.BlockSpec(memory_space=pltpu.SMEM),
            pl.BlockSpec((tile, width), lambda i: (i, 0)),
            pl.BlockSpec((width, width), lambda i: (0, 0)),
        ],
        out_specs=pl.BlockSpec((tile, width), lambda i: (i, 0)),
        compiler_params=pltpu.CompilerParams(vmem_limit_bytes=12 * 2**20),
        cost_estimate=pl.CostEstimate(flops=2 * rows * width**2, bytes_accessed=5 * 2**20, transcendentals=0),
    )(passes.reshape(1), arrived, rotation)


def prepare_kernel(
    turn, old_labels, new_labels, owner_of, slab, *refs
):
    outgoing, selection, rows_out, selection_out, row_sems, selection_sems = refs[-6:]
    rows = slab.shape[0]
    count = owner_of.shape[0]
    slots = outgoing.shape[0]
    capacity = slots // count
    tile = slots // TILES

    @pl.loop(0, turn[0])
    def _(_):
        def ints(shape, axis):
            return lax.broadcasted_iota(jnp.int32, shape, axis)

        earlier = jnp.where(ints((rows, rows), 0) < ints((rows, rows), 1), 1.0, 0.0).astype(bf16)
        names = ints((count, rows), 0)

        def rank(labels):
            named = names == labels
            before = jnp.dot(jnp.where(named, 1.0, 0.0).astype(bf16), earlier, preferred_element_type=f32)
            return jnp.sum(jnp.where(named, before, 0.0), axis=0, keepdims=True)

        old, new = old_labels[...], new_labels[...]
        owners = jnp.sum(jnp.where(names == new, owner_of[...].astype(f32), 0.0), axis=0, keepdims=True)
        old_slot = old * capacity + rank(old).astype(jnp.int32)
        new_slot = owners.astype(jnp.int32) * capacity + rank(new).astype(jnp.int32)
        copies = []
        for i in range(TILES):
            part = pl.ds(i * tile, tile)
            here = ints((tile, rows), 0) + i * tile
            marks = jnp.where(here == old_slot, 1.0, 0.0).astype(bf16)
            rows_out[i] = jnp.dot(marks, slab[...], preferred_element_type=f32).astype(bf16)
            copies.append(pltpu.make_async_copy(rows_out.at[i], outgoing.at[part], row_sems.at[i]))
            copies[-1].start()
            source = jnp.sum(jnp.where(here == new_slot, (old_slot + 1).astype(f32), 0.0), axis=1, keepdims=True) - 1.0
            chosen = ints((tile, slots), 1) == source.astype(jnp.int32)
            selection_out[i] = jnp.where(chosen, 1.0, 0.0).astype(bf16)
            copies.append(pltpu.make_async_copy(selection_out.at[i], selection.at[part], selection_sems.at[i]))
            copies[-1].start()
        for copy in copies:
            copy.wait()


def prepare(turn, old_labels, new_labels, owner_table, slab, slots, held=None):
    rows, width = slab.shape
    near, far = pl.BlockSpec(memory_space=pltpu.VMEM), pl.BlockSpec(memory_space=pltpu.HBM)
    held = () if held is None else held
    return pl.pallas_call(
        prepare_kernel,
        out_shape=[pltpu.HBM((slots, width), bf16), pltpu.HBM((slots, slots), bf16)],
        in_specs=[pl.BlockSpec(memory_space=pltpu.SMEM)] + [near] * 4 + [far] * len(held),
        out_specs=[far, far],
        input_output_aliases={5 + i: i for i in range(len(held))},
        scratch_shapes=[
            pltpu.VMEM((TILES, slots // TILES, width), bf16),
            pltpu.VMEM((TILES, slots // TILES, slots), bf16),
            pltpu.SemaphoreType.DMA((TILES,)),
            pltpu.SemaphoreType.DMA((TILES,)),
        ],
        compiler_params=pltpu.CompilerParams(vmem_limit_bytes=24 * 2**20),
        cost_estimate=pl.CostEstimate(flops=2 * slots * rows * width, bytes_accessed=5 * 2**20, transcendentals=0),
    )(turn.reshape(1), old_labels, new_labels, owner_table[:, None], slab, *held)


def shards(slab, old_cluster, new_cluster, anchor_ids, anchor_new, owner_table):
    docs_count = lax.axis_size(DOCS)
    row_count, width = slab.shape
    capacity = 2 * row_count // docs_count
    slots = docs_count * capacity
    half = anchor_ids.shape[1]
    per_source = half // docs_count
    core = lax.axis_index("rep")
    local = (old_cluster.reshape(1, row_count), new_cluster.reshape(1, row_count), owner_table, slab, slots)

    def exchange(x):
        return lax.all_to_all(x, DOCS, split_axis=0, concat_axis=0, tiled=True)

    def swap(x):
        return lax.ppermute(x, "rep", [(0, 1), (1, 0)])

    held = prepare(jnp.where(core == 0, HEAD_START, 0), *local)
    anchor_ids, held = lax.optimization_barrier((anchor_ids, held))
    asked = exchange(anchor_ids.reshape(docs_count, per_source)).reshape(-1)
    picked = select_rows(asked[:, None] == jnp.arange(row_count, dtype=jnp.int32)[None, :], slab)
    picked, held = lax.optimization_barrier((picked, held))
    fetched = exchange(picked.reshape(docs_count, per_source // 2, 2, width))
    other_new = swap(anchor_new[0])
    outgoing, selection = prepare(jnp.where(core == 0, 0, 1), *local, held)
    fetched, outgoing, other_new = lax.optimization_barrier((fetched, outgoing, other_new))
    arrived = exchange(outgoing.reshape(docs_count, capacity, width)).reshape(slots, width)

    fetched = fetched.reshape(half, width)
    other = swap(fetched)
    own_gram = jnp.einsum("ad,ae->de", fetched, anchor_new[0], preferred_element_type=f32)
    rotation = fit(own_gram, other, other_new)
    moved = map_rows(jnp.where(core == 0, MAP_PASSES, 1), arrived, rotation)

    returned = exchange(moved.reshape(docs_count, capacity, width)).reshape(slots, width)
    onward = select_rows(selection, returned)
    arrived_rows = exchange(onward.reshape(docs_count, capacity, width))
    return arrived_rows.reshape(1, slots, width)


def solution(mesh):
    docs_count, reps = mesh.devices.shape
    side = math.isqrt(docs_count // DEPTH)
    mesh = Mesh(mesh.devices.reshape(side, side, DEPTH, reps), DOCS + ("rep",))
    in_specs = (
        P(DOCS + ("rep",), None),
        P(DOCS + ("rep",), None),
        P(DOCS + ("rep",), None),
        P(DOCS, "rep"),
        P(DOCS, "rep", None),
        P(),
    )
    out_specs = P(DOCS, "rep", None)
    return jax.shard_map(shards, mesh=mesh, in_specs=in_specs, out_specs=out_specs, check_vma=False)
```

```python
import math

import jax
import jax.numpy as jnp
from jax import lax
from jax.experimental import pallas as pl
from jax.experimental.pallas import tpu as pltpu
from jax.sharding import Mesh, PartitionSpec as P

ITERS = 3
DEPTH = 8
DOCS = ("x", "y", "z")
TILES = 4
HEAD_START = 2
MAP_PASSES = 2


EPS = 1e-06
polar_scale = 0.3

bf16 = jnp.bfloat16
f32 = jnp.float32


def select_rows(marks, rows):
    return jnp.dot(marks.astype(bf16), rows, preferred_element_type=f32).astype(bf16)


def fit_kernel(own_gram, rows, targets, rotation, gram, iterate, square):
    width = own_gram.shape[0]
    gram[...] = own_gram[...] + lax.dot_general(
        rows[...], targets[...], (((0,), (0,)), ((), ())), preferred_element_type=f32
    )
    total = jnp.sum(gram[...] * gram[...])
    factor = polar_scale * math.sqrt(width) * lax.rsqrt(total + EPS)
    iterate[...] = (gram[...] * factor).astype(bf16)
    for step in range(ITERS):
        square[...] = lax.dot_general(
            iterate[...], iterate[...], (((1,), (1,)), ((), ())), preferred_element_type=f32
        ).astype(bf16)
        update = jnp.dot(square[...], iterate[...], preferred_element_type=f32)
        later = (1.5 * iterate[...].astype(f32) - 0.5 * update).astype(bf16)
        if step < ITERS - 1:
            iterate[...] = later
        else:
            rotation[...] = later


def fit(own_gram, rows, targets):
    width = own_gram.shape[0]
    whole = pl.BlockSpec(memory_space=pltpu.VMEM)
    return pl.pallas_call(
        fit_kernel,
        out_shape=jax.ShapeDtypeStruct((width, width), bf16),
        in_specs=[whole] * 3,
        out_specs=whole,
        scratch_shapes=[
            pltpu.VMEM((width, width), f32),
            pltpu.VMEM((width, width), bf16),
            pltpu.VMEM((width, width), bf16),
        ],
        compiler_params=pltpu.CompilerParams(vmem_limit_bytes=32 * 2**20),
        cost_estimate=pl.CostEstimate(
            flops=2 * (rows.shape[0] * width**2 + 2 * ITERS * width**3), bytes_accessed=6 * 2**20, transcendentals=1
        ),
    )(own_gram, rows, targets)


def map_kernel(passes, arrived, rotation, moved):
    @pl.loop(0, passes[0])
    def _(_):
        moved[...] = jnp.dot(arrived[...], rotation[...], preferred_element_type=f32).astype(bf16)


def map_rows(passes, arrived, rotation):
    rows, width = arrived.shape
    tile = rows // TILES
    return pl.pallas_call(
        map_kernel,
        grid=(TILES,),
        out_shape=pltpu.HBM((rows, width), bf16),
        in_specs=[
            pl.BlockSpec(memory_space=pltpu.SMEM),
            pl.BlockSpec((tile, width), lambda i: (i, 0)),
            pl.BlockSpec((width, width), lambda i: (0, 0)),
        ],
        out_specs=pl.BlockSpec((tile, width), lambda i: (i, 0)),
        compiler_params=pltpu.CompilerParams(vmem_limit_bytes=12 * 2**20),
        cost_estimate=pl.CostEstimate(flops=2 * rows * width**2, bytes_accessed=5 * 2**20, transcendentals=0),
    )(passes.reshape(1), arrived, rotation)


def prepare_kernel(turn, old_ref, new_ref, owner_ref, slab_ref, *refs):
    outgoing, selection, old_row, new_row, owner_of, slab, rows_out, selection_out, fetch_sems, row_sems, selection_sems = refs[-11:]
    rows = slab.shape[0]
    count = owner_of.shape[1]
    slots = outgoing.shape[0]
    capacity = slots // count
    tile = slots // TILES

    @pl.loop(0, turn[0])
    def _(_):
        fetches = [
            pltpu.make_async_copy(source, target, fetch_sems.at[i])
            for i, (source, target) in enumerate(
                ((old_ref, old_row), (new_ref, new_row), (owner_ref, owner_of), (slab_ref, slab))
            )
        ]
        for fetch in fetches:
            fetch.start()
        for fetch in fetches:
            fetch.wait()

        def ints(shape, axis):
            return lax.broadcasted_iota(jnp.int32, shape, axis)

        earlier = jnp.where(ints((rows, rows), 0) < ints((rows, rows), 1), 1.0, 0.0).astype(bf16)
        names = ints((count, rows), 0)

        def named(labels):
            return jnp.where(names == labels, 1.0, 0.0)

        def rank(marks):
            before = jnp.dot(marks.astype(bf16), earlier, preferred_element_type=f32)
            return jnp.sum(marks * before, axis=0, keepdims=True).astype(jnp.int32)

        old, new = old_row[...], new_row[...]
        old_marks, new_marks = named(old), named(new)
        table = jnp.broadcast_to(owner_of[...].astype(f32), (8, count)).astype(bf16)
        owners = jnp.dot(table, new_marks.astype(bf16), preferred_element_type=f32)[:1].astype(jnp.int32)
        old_slot = old * capacity + rank(old_marks)
        new_slot = owners * capacity + rank(new_marks)
        copies = []
        for i in range(TILES):
            part = pl.ds(i * tile, tile)
            here = ints((tile, rows), 0) + i * tile
            marks = jnp.where(here == old_slot, 1.0, 0.0).astype(bf16)
            rows_out[i] = jnp.dot(marks, slab[...], preferred_element_type=f32).astype(bf16)
            copies.append(pltpu.make_async_copy(rows_out.at[i], outgoing.at[part], row_sems.at[i]))
            copies[-1].start()
            source = jnp.sum(jnp.where(here == new_slot, (old_slot + 1).astype(f32), 0.0), axis=1, keepdims=True) - 1.0
            chosen = ints((tile, slots), 1) == source.astype(jnp.int32)
            selection_out[i] = jnp.where(chosen, 1.0, 0.0).astype(bf16)
            copies.append(pltpu.make_async_copy(selection_out.at[i], selection.at[part], selection_sems.at[i]))
            copies[-1].start()
        for copy in copies:
            copy.wait()


def prepare(turn, old_labels, new_labels, owner_table, slab, slots, held=()):
    rows, width = slab.shape
    count = owner_table.shape[0]
    far = pl.BlockSpec(memory_space=pl.ANY)
    return pl.pallas_call(
        prepare_kernel,
        out_shape=[pltpu.HBM((slots, width), bf16), pltpu.HBM((slots, slots), bf16)],
        in_specs=[pl.BlockSpec(memory_space=pltpu.SMEM)] + [far] * (4 + len(held)),
        out_specs=[pl.BlockSpec(memory_space=pltpu.HBM)] * 2,
        input_output_aliases={5 + i: i for i in range(len(held))},
        scratch_shapes=[
            pltpu.VMEM((1, rows), jnp.int32),
            pltpu.VMEM((1, rows), jnp.int32),
            pltpu.VMEM((1, count), jnp.int32),
            pltpu.VMEM((rows, width), bf16),
            pltpu.VMEM((TILES, slots // TILES, width), bf16),
            pltpu.VMEM((TILES, slots // TILES, slots), bf16),
            pltpu.SemaphoreType.DMA((4,)),
            pltpu.SemaphoreType.DMA((TILES,)),
            pltpu.SemaphoreType.DMA((TILES,)),
        ],
        compiler_params=pltpu.CompilerParams(vmem_limit_bytes=60 * 2**20),
        cost_estimate=pl.CostEstimate(flops=2 * slots * rows * width, bytes_accessed=5 * 2**20, transcendentals=0),
    )(turn.reshape(1), old_labels, new_labels, owner_table.reshape(1, count), slab, *held)


def shards(slab, old_cluster, new_cluster, anchor_ids, anchor_new, owner_table):
    docs_count = lax.axis_size(DOCS)
    row_count, width = slab.shape
    capacity = 2 * row_count // docs_count
    slots = docs_count * capacity
    half = anchor_ids.shape[1]
    per_source = half // docs_count
    core = lax.axis_index("rep")
    local = (old_cluster.reshape(1, row_count), new_cluster.reshape(1, row_count), owner_table, slab, slots)

    def exchange(x):
        return lax.all_to_all(x, DOCS, split_axis=0, concat_axis=0, tiled=True)

    def swap(x):
        return lax.ppermute(x, "rep", [(0, 1), (1, 0)])

    held = prepare(jnp.where(core == 0, HEAD_START, 0), *local)
    anchor_ids, held = lax.optimization_barrier((anchor_ids, held))
    asked = exchange(anchor_ids.reshape(docs_count, per_source)).reshape(-1)
    picked = select_rows(asked[:, None] == jnp.arange(row_count, dtype=jnp.int32)[None, :], slab)
    picked, held = lax.optimization_barrier((picked, held))
    fetched = exchange(picked.reshape(docs_count, per_source // 2, 2, width)).reshape(half, width)
    other_new = swap(anchor_new[0])
    outgoing, selection = prepare(jnp.where(core == 0, 0, 1), *local, held)
    fetched, outgoing, other_new = lax.optimization_barrier((fetched, outgoing, other_new))
    arrived = exchange(outgoing.reshape(docs_count, capacity, width)).reshape(slots, width)

    other = swap(fetched)
    own_gram = jnp.einsum("ad,ae->de", fetched, anchor_new[0], preferred_element_type=f32)
    rotation = fit(own_gram, other, other_new)
    moved = map_rows(jnp.where(core == 0, MAP_PASSES, 1), arrived, rotation)

    returned = exchange(moved.reshape(docs_count, capacity, width)).reshape(slots, width)
    onward = select_rows(selection, returned)
    arrived_rows = exchange(onward.reshape(docs_count, capacity, width))
    return arrived_rows.reshape(1, slots, width)


def solution(mesh):
    docs_count, reps = mesh.devices.shape
    side = math.isqrt(docs_count // DEPTH)
    mesh = Mesh(mesh.devices.reshape(side, side, DEPTH, reps), DOCS + ("rep",))
    in_specs = (
        P(DOCS + ("rep",), None),
        P(DOCS + ("rep",), None),
        P(DOCS + ("rep",), None),
        P(DOCS, "rep"),
        P(DOCS, "rep", None),
        P(),
    )
    out_specs = P(DOCS, "rep", None)
    return jax.shard_map(shards, mesh=mesh, in_specs=in_specs, out_specs=out_specs, check_vma=False)
```

```python
import math

import jax
import jax.numpy as jnp
from jax import lax
from jax.experimental import pallas as pl
from jax.experimental.pallas import tpu as pltpu
from jax.sharding import Mesh, PartitionSpec as P

ITERS = 3
DEPTH = 8
DOCS = ("x", "y", "z")
TILES = 4
HEAD_START = 2
MAP_PASSES = 2


EPS = 1e-06
polar_scale = 0.3

bf16 = jnp.bfloat16
f32 = jnp.float32


def select_rows(marks, rows):
    return jnp.dot(marks.astype(bf16), rows, preferred_element_type=f32).astype(bf16)


def fit_kernel(own_gram, rows, targets, rotation, gram, iterate, square):
    width = own_gram.shape[0]
    gram[...] = own_gram[...] + lax.dot_general(
        rows[...], targets[...], (((0,), (0,)), ((), ())), preferred_element_type=f32
    )
    total = jnp.sum(gram[...] * gram[...])
    factor = polar_scale * math.sqrt(width) * lax.rsqrt(total + EPS)
    iterate[...] = (gram[...] * factor).astype(bf16)
    for step in range(ITERS):
        square[...] = lax.dot_general(
            iterate[...], iterate[...], (((1,), (1,)), ((), ())), preferred_element_type=f32
        ).astype(bf16)
        update = jnp.dot(square[...], iterate[...], preferred_element_type=f32)
        later = (1.5 * iterate[...].astype(f32) - 0.5 * update).astype(bf16)
        if step < ITERS - 1:
            iterate[...] = later
        else:
            rotation[...] = later


def fit(own_gram, rows, targets):
    width = own_gram.shape[0]
    whole = pl.BlockSpec(memory_space=pltpu.VMEM)
    return pl.pallas_call(
        fit_kernel,
        out_shape=jax.ShapeDtypeStruct((width, width), bf16),
        in_specs=[whole] * 3,
        out_specs=whole,
        scratch_shapes=[
            pltpu.VMEM((width, width), f32),
            pltpu.VMEM((width, width), bf16),
            pltpu.VMEM((width, width), bf16),
        ],
        compiler_params=pltpu.CompilerParams(vmem_limit_bytes=32 * 2**20),
        cost_estimate=pl.CostEstimate(
            flops=2 * (rows.shape[0] * width**2 + 2 * ITERS * width**3), bytes_accessed=6 * 2**20, transcendentals=1
        ),
    )(own_gram, rows, targets)


def map_kernel(passes, arrived, rotation, moved):
    @pl.loop(0, passes[0])
    def _(_):
        moved[...] = jnp.dot(arrived[...], rotation[...], preferred_element_type=f32).astype(bf16)


def map_rows(passes, arrived, rotation):
    rows, width = arrived.shape
    tile = rows // 2
    return pl.pallas_call(
        map_kernel,
        grid=(2,),
        out_shape=pltpu.HBM((rows, width), bf16),
        in_specs=[
            pl.BlockSpec(memory_space=pltpu.SMEM),
            pl.BlockSpec((tile, width), lambda i: (i, 0)),
            pl.BlockSpec((width, width), lambda i: (0, 0)),
        ],
        out_specs=pl.BlockSpec((tile, width), lambda i: (i, 0)),
        compiler_params=pltpu.CompilerParams(vmem_limit_bytes=24 * 2**20),
        cost_estimate=pl.CostEstimate(flops=2 * rows * width**2, bytes_accessed=5 * 2**20, transcendentals=0),
    )(passes.reshape(1), arrived, rotation)


def prepare_kernel(turn, old_ref, new_ref, owner_ref, slab_ref, *refs):
    outgoing, selection, old_row, new_row, owner_of, slab, rows_out, selection_out, fetch_sems, row_sems, selection_sems = refs[-11:]
    rows = slab.shape[0]
    count = owner_of.shape[1]
    slots = outgoing.shape[0]
    capacity = slots // count
    tile = slots // TILES

    @pl.loop(0, turn[0])
    def _(_):
        fetches = [
            pltpu.make_async_copy(source, target, fetch_sems.at[i])
            for i, (source, target) in enumerate(
                ((old_ref, old_row), (new_ref, new_row), (owner_ref, owner_of), (slab_ref, slab))
            )
        ]
        for fetch in fetches:
            fetch.start()
        for fetch in fetches:
            fetch.wait()

        def ints(shape, axis):
            return lax.broadcasted_iota(jnp.int32, shape, axis)

        earlier = jnp.where(ints((rows, rows), 0) < ints((rows, rows), 1), 1.0, 0.0).astype(bf16)
        names = ints((count, rows), 0)

        def named(labels):
            return jnp.where(names == labels, 1.0, 0.0)

        def rank(marks):
            before = jnp.dot(marks.astype(bf16), earlier, preferred_element_type=f32)
            return jnp.sum(marks * before, axis=0, keepdims=True).astype(jnp.int32)

        old, new = old_row[...], new_row[...]
        old_marks, new_marks = named(old), named(new)
        table = jnp.broadcast_to(owner_of[...].astype(f32), (8, count)).astype(bf16)
        owners = jnp.dot(table, new_marks.astype(bf16), preferred_element_type=f32)[:1].astype(jnp.int32)
        old_slot = old * capacity + rank(old_marks)
        new_slot = owners * capacity + rank(new_marks)
        copies = []
        for i in range(TILES):
            part = pl.ds(i * tile, tile)
            here = ints((tile, rows), 0) + i * tile
            marks = jnp.where(here == old_slot, 1.0, 0.0).astype(bf16)
            rows_out[i] = jnp.dot(marks, slab[...], preferred_element_type=f32).astype(bf16)
            copies.append(pltpu.make_async_copy(rows_out.at[i], outgoing.at[part], row_sems.at[i]))
            copies[-1].start()
            source = jnp.sum(jnp.where(here == new_slot, (old_slot + 1).astype(f32), 0.0), axis=1, keepdims=True) - 1.0
            chosen = ints((tile, slots), 1) == source.astype(jnp.int32)
            selection_out[i] = jnp.where(chosen, 1.0, 0.0).astype(bf16)
            copies.append(pltpu.make_async_copy(selection_out.at[i], selection.at[part], selection_sems.at[i]))
            copies[-1].start()
        for copy in copies:
            copy.wait()


def prepare(turn, old_labels, new_labels, owner_table, slab, slots, held=()):
    rows, width = slab.shape
    count = owner_table.shape[0]
    far = pl.BlockSpec(memory_space=pl.ANY)
    return pl.pallas_call(
        prepare_kernel,
        out_shape=[pltpu.HBM((slots, width), bf16), pltpu.HBM((slots, slots), bf16)],
        in_specs=[pl.BlockSpec(memory_space=pltpu.SMEM)] + [far] * (4 + len(held)),
        out_specs=[pl.BlockSpec(memory_space=pltpu.HBM)] * 2,
        input_output_aliases={5 + i: i for i in range(len(held))},
        scratch_shapes=[
            pltpu.VMEM((1, rows), jnp.int32),
            pltpu.VMEM((1, rows), jnp.int32),
            pltpu.VMEM((1, count), jnp.int32),
            pltpu.VMEM((rows, width), bf16),
            pltpu.VMEM((TILES, slots // TILES, width), bf16),
            pltpu.VMEM((TILES, slots // TILES, slots), bf16),
            pltpu.SemaphoreType.DMA((4,)),
            pltpu.SemaphoreType.DMA((TILES,)),
            pltpu.SemaphoreType.DMA((TILES,)),
        ],
        compiler_params=pltpu.CompilerParams(vmem_limit_bytes=60 * 2**20),
        cost_estimate=pl.CostEstimate(flops=2 * slots * rows * width, bytes_accessed=5 * 2**20, transcendentals=0),
    )(turn.reshape(1), old_labels, new_labels, owner_table.reshape(1, count), slab, *held)


def shards(slab, old_cluster, new_cluster, anchor_ids, anchor_new, owner_table):
    docs_count = lax.axis_size(DOCS)
    row_count, width = slab.shape
    capacity = 2 * row_count // docs_count
    slots = docs_count * capacity
    half = anchor_ids.shape[1]
    per_source = half // docs_count
    core = lax.axis_index("rep")
    local = (old_cluster.reshape(1, row_count), new_cluster.reshape(1, row_count), owner_table, slab, slots)

    def exchange(x):
        return lax.all_to_all(x, DOCS, split_axis=0, concat_axis=0, tiled=True)

    def swap(x):
        return lax.ppermute(x, "rep", [(0, 1), (1, 0)])

    held = prepare(jnp.where(core == 0, HEAD_START, 0), *local)
    anchor_ids, held = lax.optimization_barrier((anchor_ids, held))
    asked = exchange(anchor_ids.reshape(docs_count, per_source)).reshape(-1)
    picked = select_rows(asked[:, None] == jnp.arange(row_count, dtype=jnp.int32)[None, :], slab)
    picked, held = lax.optimization_barrier((picked, held))
    fetched = exchange(picked.reshape(docs_count, per_source // 2, 2, width)).reshape(half, width)
    other_new = swap(anchor_new[0])
    outgoing, selection = prepare(jnp.where(core == 0, 0, 1), *local, held)
    fetched, outgoing, other_new = lax.optimization_barrier((fetched, outgoing, other_new))
    arrived = exchange(outgoing.reshape(docs_count, capacity, width)).reshape(slots, width)

    other = swap(fetched)
    own_gram = jnp.einsum("ad,ae->de", fetched, anchor_new[0], preferred_element_type=f32)
    rotation = fit(own_gram, other, other_new)
    moved = map_rows(jnp.where(core == 0, MAP_PASSES, 1), arrived, rotation)

    returned = exchange(moved.reshape(docs_count, capacity, width)).reshape(slots, width)
    onward = select_rows(selection, returned)
    arrived_rows = exchange(onward.reshape(docs_count, capacity, width))
    return arrived_rows.reshape(1, slots, width)


def solution(mesh):
    docs_count, reps = mesh.devices.shape
    side = math.isqrt(docs_count // DEPTH)
    mesh = Mesh(mesh.devices.reshape(side, side, DEPTH, reps), DOCS + ("rep",))
    in_specs = (
        P(DOCS + ("rep",), None),
        P(DOCS + ("rep",), None),
        P(DOCS + ("rep",), None),
        P(DOCS, "rep"),
        P(DOCS, "rep", None),
        P(),
    )
    out_specs = P(DOCS, "rep", None)
    return jax.shard_map(shards, mesh=mesh, in_specs=in_specs, out_specs=out_specs, check_vma=False)
```
